32 devices in a mesh: row: 8 (over z, core), col: 4 (over y, x).
Axes of the slice: x: 2, y: 2, z: 4, core: 2. Of those that a mesh axis runs over, the one named last changes fastest.
Arguments:
- left_blocks: bfloat16 [8, 4, 4, 256, 256], P('row', 'col'), may hold values from -6 to 6
- left_rows: int32 [8, 4, 4], P('row', 'col'), may hold values from 0 to 15, as said below
- left_cols: int32 [8, 4, 4], P('row', 'col'), may hold values from 0 to 31, as said below
- left_count: int32 [8, 4], P('row', 'col'), may hold values from 1 to 4, as said below
- right_blocks: bfloat16 [8, 4, 1, 256, 256], P('row', 'col'), may hold values from -0.375 to 0.375
- right_rows: int32 [8, 4, 1], P('row', 'col'), may hold values from 0 to 15, as said below
- right_cols: int32 [8, 4, 1], P('row', 'col'), may hold values from 0 to 31, as said below
- kept_rows: int32 [8, 2], P('row'), may hold values from 0 to 15, as said below
- kept_cols: int32 [4, 4], P('col'), may hold values from 0 to 31, as said below
Outputs:
- product: bfloat16 [8, 4, 2, 4, 256, 256], P('row', 'col')
The draws below stay inside these ranges and needn't reach their ends.
Inputs may be any that keep to these rules, and one draw needn't show every extreme that they name: `left_rows`: each entry is one of the 2 entries of kept_rows for its row panel. For a slot of contraction panel k, left_cols = u * 16 + v with u 0 or 1, where v is one of the block rows that right_rows lists for sub-panel 2 * k + u (the same on every column panel). `left_count`: slots at or past the count are unused and hold arbitrary blocks and indices; some panel uses all 4 slots. `right_rows`: all column panels of one sub-panel list the same 1 distinct block rows. `right_cols`: each entry is one of the 4 entries of kept_cols for its column panel. `kept_rows`: distinct within a row panel. `kept_cols`: distinct within a column panel.
All inputs are finite; a program needn't handle non-finite values.
Results may differ from the reference program's by a relative error of at most 0.001.
Values may be sent and summed in bfloat16 or wider, within the bound.
A program may use at most 64 MiB of HBM per device.

```python
import jax
import jax.numpy as jnp
from jax import lax

BS = 256
RB = 16
SA = 4
SB = 1
RA = 2
CA = 4
CB = 32
ROW_PANELS = 8
COL_PANELS = 4


def layout(key):
    streams = jax.random.split(jax.random.fold_in(key, 7), 8)
    kept_rows = jax.vmap(lambda single: jax.random.permutation(single, RB)[:RA])(jax.random.split(streams[0], ROW_PANELS)).astype(jnp.int32)
    kept_cols = jax.vmap(lambda single: jax.random.permutation(single, CB)[:CA])(jax.random.split(streams[1], COL_PANELS)).astype(jnp.int32)
    active = jax.vmap(lambda single: jax.random.permutation(single, RB)[:SB])(jax.random.split(streams[2], ROW_PANELS)).astype(jnp.int32)
    right_rows = jnp.broadcast_to(active[:, None, :], (ROW_PANELS, COL_PANELS, SB))
    pick_col = jax.random.randint(streams[3], (ROW_PANELS, COL_PANELS, SB), 0, CA)
    right_cols = jnp.take_along_axis(jnp.broadcast_to(kept_cols[None, :, :], (ROW_PANELS, COL_PANELS, CA)), pick_col, axis=2).astype(jnp.int32)
    pick_row = jax.random.randint(streams[4], (ROW_PANELS, COL_PANELS, SA), 0, RA)
    left_rows = jnp.take_along_axis(jnp.broadcast_to(kept_rows[:, None, :], (ROW_PANELS, COL_PANELS, RA)), pick_row, axis=2).astype(jnp.int32)
    half_pick = jax.random.randint(streams[5], (ROW_PANELS, COL_PANELS, SA), 0, 2)
    slot_pick = jax.random.randint(streams[6], (ROW_PANELS, COL_PANELS, SA), 0, SB)
    panel_ids = jnp.arange(COL_PANELS, dtype=jnp.int32)[None, :, None]
    sub_panel = 2 * panel_ids + half_pick
    left_cols = (half_pick * RB + active.reshape(-1)[sub_panel * SB + slot_pick]).astype(jnp.int32)
    left_count = jax.random.randint(streams[7], (ROW_PANELS, COL_PANELS), 1, SA + 1).at[0, 0].set(SA).astype(jnp.int32)
    return (left_rows, left_cols, left_count, right_rows, right_cols, kept_rows, kept_cols)


def draw_left_rows(key, part):
    return layout(key)[0]


def draw_left_cols(key, part):
    return layout(key)[1]


def draw_left_count(key, part):
    return layout(key)[2]


def draw_right_rows(key, part):
    return layout(key)[3]


def draw_right_cols(key, part):
    return layout(key)[4]


def draw_kept_rows(key, part):
    return layout(key)[5]


def draw_kept_cols(key, part):
    return layout(key)[6]


def steps_of(rng, extent, cuts, least, top_value):
    gain = 1.0
    for axis_at, shards_of in cuts:
        draws = jax.random.uniform(jax.random.fold_in(jax.random.fold_in(rng, 6), axis_at), (shards_of,), jnp.float32, least / len(cuts), top_value / len(cuts))
        gain = gain * jnp.repeat(jnp.exp(draws), extent[axis_at] // shards_of).reshape((-1,) + (1,) * (len(extent) - 1 - axis_at))
    return gain


def noise(stream_key, extent, scale, reach, pieces=(), kind=jnp.bfloat16):
    drawn = jax.random.normal(stream_key, extent, jnp.float32) * scale
    if len(pieces) > 0:
        drawn = steps_of(stream_key, extent, pieces, -0.22, 0.18) * drawn
    return jnp.clip(drawn, min=-reach, max=reach).astype(kind)


def setup_inputs(seed: int = 0) -> dict:
    arg_keys = jax.random.split(jax.random.key(seed), 10)
    left_blocks = noise(arg_keys[0], (ROW_PANELS, COL_PANELS, SA, BS, BS), 1.0, 6.0, ((0, 8), (1, 4)))
    left_rows = draw_left_rows(jax.random.fold_in(arg_keys[9], 71), 0)
    left_cols = draw_left_cols(jax.random.fold_in(arg_keys[9], 71), 0)
    left_count = draw_left_count(jax.random.fold_in(arg_keys[9], 71), 0)
    right_blocks = noise(arg_keys[4], (ROW_PANELS, COL_PANELS, SB, BS, BS), BS ** -0.5, 0.375, ((0, 8), (1, 4)))
    right_rows = draw_right_rows(jax.random.fold_in(arg_keys[9], 71), 0)
    right_cols = draw_right_cols(jax.random.fold_in(arg_keys[9], 71), 0)
    kept_rows = draw_kept_rows(jax.random.fold_in(arg_keys[9], 71), 0)
    kept_cols = draw_kept_cols(jax.random.fold_in(arg_keys[9], 71), 0)
    return {"left_blocks": left_blocks, "left_rows": left_rows, "left_cols": left_cols, "left_count": left_count, "right_blocks": right_blocks, "right_rows": right_rows, "right_cols": right_cols, "kept_rows": kept_rows, "kept_cols": kept_cols}


def device_block(flat_index, left_blocks, left_rows, left_cols, left_count, right_blocks, right_rows, right_cols, kept_rows, kept_cols):
    row_panel = flat_index // COL_PANELS
    col_panel = flat_index % COL_PANELS
    halves = ROW_PANELS // COL_PANELS
    left_panel = left_blocks[row_panel].astype(jnp.float32)
    right_panel = right_blocks[:, col_panel].astype(jnp.float32).reshape(COL_PANELS, halves, SB, BS, BS)
    offsets = (RB * jnp.arange(halves)).astype(jnp.int32)
    right_contract = right_rows[:, col_panel].reshape(COL_PANELS, halves, SB) + offsets[None, :, None]
    right_column = right_cols[:, col_panel].reshape(COL_PANELS, halves, SB)
    live_slot = jnp.arange(SA).astype(jnp.int32)[None, :] < left_count[row_panel][:, None]
    matched = (left_cols[row_panel][:, :, None, None] == right_contract[:, None, :, :]) & live_slot[:, :, None, None]
    row_hit = left_rows[row_panel][:, :, None] == kept_rows[row_panel][None, None, :]
    col_hit = right_column[:, :, :, None] == kept_cols[col_panel][None, None, None, :]
    weights = (matched[:, :, :, :, None, None] & row_hit[:, :, None, None, :, None] & col_hit[:, None, :, :, None, :]).astype(jnp.float32)
    products = jnp.einsum("kamn,kubnp->kaubmp", left_panel, right_panel, precision=lax.Precision.HIGHEST)
    summed = jnp.einsum("kaubij,kaubmp->ijmp", weights, products, precision=lax.Precision.HIGHEST)
    return summed.astype(jnp.bfloat16)


def reference(left_blocks, left_rows, left_cols, left_count, right_blocks, right_rows, right_cols, kept_rows, kept_cols):
    indices = jnp.arange(ROW_PANELS * COL_PANELS).astype(jnp.int32)
    stacked = lax.map(lambda flat_index: device_block(flat_index, left_blocks, left_rows, left_cols, left_count, right_blocks, right_rows, right_cols, kept_rows, kept_cols), indices)
    return stacked.reshape(ROW_PANELS, COL_PANELS, RA, CA, BS, BS)
```

```python
import functools

import jax
import jax.numpy as jnp
from jax import lax
from jax.experimental import pallas as pl
from jax.experimental.pallas import tpu as pltpu
from jax.sharding import PartitionSpec as P

RB = 16


def flip(index, mask):
    bit = 1
    moved = index
    while bit <= mask:
        if mask & bit:
            moved = moved + bit - 2 * bit * ((index // bit) % 2)
        bit *= 2
    return moved


def kernel(
    nr,
    nc,
    left_ref,
    lrows,
    lcols,
    lcount,
    right_ref,
    rrows,
    rcols,
    krows,
    kcols,
    out_ref,
    lefts,
    rights,
    sums,
    stage,
    meta_l,
    meta_r,
    small_l,
    small_r,
    l_send,
    l_recv,
    f_send,
    r_send,
    r_recv,
    ml_send,
    ml_recv,
    mr_send,
    mr_recv,
    own_sem,
    small_sem,
    out_sem,
):
    me_r = lax.axis_index("row")
    me_c = lax.axis_index("col")
    slots = left_ref.shape[2]
    depth = right_ref.shape[2]
    halves = nr // nc
    keep_r = krows.shape[1]
    keep_c = kcols.shape[1]

    own_left = pltpu.make_async_copy(left_ref.at[0, 0], lefts.at[me_c], own_sem.at[0])
    own_right = pltpu.make_async_copy(
        right_ref.at[0, 0], rights.at[pl.ds(me_r * depth, depth)], own_sem.at[1]
    )
    own_left.start()
    own_right.start()

    barrier = pltpu.get_barrier_semaphore()
    for p in range(1, nc):
        pl.semaphore_signal(
            barrier, inc=1, device_id={"col": flip(me_c, p)}, device_id_type=pl.DeviceIdType.MESH
        )
    for p in range(1, nr):
        pl.semaphore_signal(
            barrier, inc=1, device_id={"row": flip(me_r, p)}, device_id_type=pl.DeviceIdType.MESH
        )

    lane = lax.broadcasted_iota(jnp.int32, meta_l.shape[1:], 1)
    tile = jnp.zeros(meta_l.shape[1:], jnp.int32)
    for a in range(slots):
        tile = jnp.where(lane == a, lrows[0, 0, a], tile)
        tile = jnp.where(lane == slots + a, lcols[0, 0, a], tile)
    tile = jnp.where(lane == 2 * slots, lcount[0, 0], tile)
    base = 2 * slots + 1
    for b in range(depth):
        tile = jnp.where(lane == base + b, rrows[0, 0, b], tile)
        tile = jnp.where(lane == base + depth + b, rcols[0, 0, b], tile)
    meta_l[me_c] = tile
    meta_r[me_r] = tile
    sums[0] = jnp.zeros(sums.shape[1:], sums.dtype)

    pl.semaphore_wait(barrier, nc - 1 + nr - 1)

    def along(axis, peer, src, dst, send, recv):
        return pltpu.make_async_remote_copy(
            src_ref=src,
            dst_ref=dst,
            send_sem=send,
            recv_sem=recv,
            device_id={axis: peer},
            device_id_type=pl.DeviceIdType.MESH,
        )

    sent = []

    relayed = nc % 4 == 0
    half = slots // 2
    first = list(range(half))
    second = list(range(half, slots))
    relay_of = {1: first, 2: second}

    def send_left(p, a):
        copy = along(
            "col",
            flip(me_c, p),
            left_ref.at[0, 0, a],
            lefts.at[me_c, a],
            l_send.at[p, a],
            l_recv.at[p, a],
        )
        copy.start()
        sent.append(copy)

    if relayed:
        for a, b in zip(first + second, second + first) if len(first) == len(second) else []:
            send_left(1, a)
            send_left(2, b)
        if len(first) != len(second):
            for a in first + second:
                send_left(1, a)
            for a in second + first:
                send_left(2, a)
        direct = [p for p in range(4, nc)]
    else:
        direct = [p for p in range(1, nc)]

    def rows_of(q):
        return rights.at[pl.ds(q * depth, depth)]

    for p in [p for p in range(2, nr, 2)] + [1]:
        copy = along(
            "row",
            flip(me_r, p),
            right_ref.at[0, 0],
            rows_of(me_r),
            r_send.at[p],
            r_recv.at[p],
        )
        copy.start()
        sent.append(copy)
    for p in range(1, nr):
        copy = along(
            "row", flip(me_r, p), meta_r.at[me_r], meta_r.at[me_r], mr_send.at[p], mr_recv.at[p]
        )
        copy.start()
        sent.append(copy)
    for p in range(1, nc):
        copy = along(
            "col", flip(me_c, p), meta_l.at[me_c], meta_l.at[me_c], ml_send.at[p], ml_recv.at[p]
        )
        copy.start()
        sent.append(copy)
    for p in direct:
        for a in range(slots):
            send_left(p, a)

    def wait_left(p, a):
        k = flip(me_c, p)
        along(
            "col", k, lefts.at[k, a], lefts.at[k, a], l_send.at[p, a], l_recv.at[p, a]
        ).wait_recv()

    def wait_right(p):
        q = flip(me_r, p)
        along("row", q, rows_of(q), rows_of(q), r_send.at[p], r_recv.at[p]).wait_recv()

    waited = set()

    def pass_left(p, a):
        wait_left(p, a)
        waited.add((p, a))
        k = flip(me_c, p)
        copy = along(
            "col",
            flip(me_c, 3 - p),
            lefts.at[k, a],
            lefts.at[k, a],
            f_send.at[a],
            l_recv.at[3, a],
        )
        copy.start()
        sent.append(copy)

    def pass_right(p):
        wait_right(p)
        q = flip(me_r, p)
        copy = along("row", flip(me_r, 1), rows_of(q), rows_of(q), r_send.at[p + 1], r_recv.at[p + 1])
        copy.start()
        sent.append(copy)

    left_steps = []
    if relayed:
        for n in range(max(len(first), len(second))):
            for p in (1, 2):
                if n < len(relay_of[p]):
                    left_steps.append(functools.partial(pass_left, p, relay_of[p][n]))
    right_steps = [functools.partial(pass_right, p) for p in range(2, nr, 2)]
    while left_steps or right_steps:
        for step in left_steps[:2] + right_steps[:1]:
            step()
        left_steps, right_steps = left_steps[2:], right_steps[1:]

    for p in range(1, nr):
        q = flip(me_r, p)
        along("row", q, meta_r.at[q], meta_r.at[q], mr_send.at[p], mr_recv.at[p]).wait_recv()
    for p in range(1, nc):
        k = flip(me_c, p)
        along("col", k, meta_l.at[k], meta_l.at[k], ml_send.at[p], ml_recv.at[p]).wait_recv()
    to_small = [
        pltpu.make_async_copy(meta_l, small_l, small_sem.at[0]),
        pltpu.make_async_copy(meta_r, small_r, small_sem.at[1]),
    ]
    for copy in to_small:
        copy.start()
    for copy in to_small:
        copy.wait()

    order = [(0, a) for a in range(slots)]
    if relayed:
        order += [(1, a) for a in first] + [(2, a) for a in second]
        order += [(1, a) for a in second] + [(2, a) for a in first]
        for a, b in zip(first, second):
            order += [(3, a), (3, b)]
        order += [(3, a) for a in first[len(second) :] + second[len(first) :]]
    order += [(p, a) for p in direct for a in range(slots)]

    last = {(i, j): jnp.int32(0) for i in range(keep_r) for j in range(keep_c)}
    plan = []
    for t, (p, a) in enumerate(order):
        k = flip(me_c, p)
        row = small_l[k, 0, a]
        contract = small_l[k, 0, slots + a]
        live = a < small_l[k, 0, 2 * slots]
        source = jnp.int32(0)
        column = jnp.int32(-1)
        for u in range(halves):
            q = halves * k + u
            for b in range(depth):
                match = contract == u * RB + small_r[q, 0, base + b]
                source = jnp.where(match, q * depth + b, source)
                column = jnp.where(match, small_r[q, 0, base + depth + b], column)
        before = jnp.int32(0)
        for i in range(keep_r):
            row_on = live & (row == krows[0, i])
            for j in range(keep_c):
                on = row_on & (column == kcols[0, j])
                before = jnp.where(on, last[i, j], before)
                last[i, j] = jnp.where(on, t + 1, last[i, j])
        plan.append((k, source, before))

    own_right.wait()
    for p in [1] + [p for p in range(3, nr, 2)]:
        wait_right(p)
    own_left.wait()
    for t, (p, a) in enumerate(order):
        if p > 0 and (p, a) not in waited:
            wait_left(p, a)
        k, source, before = plan[t]
        sums[t + 1] = sums[before] + jnp.dot(
            lefts[k, a], rights[source], preferred_element_type=jnp.float32
        )

    outs = []
    for i in range(keep_r):
        for j in range(keep_c):
            stage[i, j] = sums[last[i, j]].astype(stage.dtype)
            copy = pltpu.make_async_copy(
                stage.at[i, j], out_ref.at[0, 0, i, j], out_sem.at[i * keep_c + j]
            )
            copy.start()
            outs.append(copy)
    for copy in sent:
        copy.wait_send()
    for copy in outs:
        copy.wait()


def solution(mesh):
    nr, nc = mesh.shape["row"], mesh.shape["col"]

    def body(
        left_blocks,
        left_rows,
        left_cols,
        left_count,
        right_blocks,
        right_rows,
        right_cols,
        kept_rows,
        kept_cols,
    ):
        slots, width = left_blocks.shape[2], left_blocks.shape[3]
        depth = right_blocks.shape[2]
        keep_r, keep_c = kept_rows.shape[1], kept_cols.shape[1]
        kind = left_blocks.dtype
        block = width * width
        vmem = (
            2 * block * (nc * slots + nr * depth + keep_r * keep_c)
            + 4 * block * (nc * slots + 1)
            + 4 * 1024 * (nr + nc)
            + (4 << 20)
        )
        small = pl.BlockSpec(memory_space=pltpu.SMEM)
        large = pl.BlockSpec(memory_space=pl.ANY)
        dma = pltpu.SemaphoreType.DMA
        return pl.pallas_call(
            functools.partial(kernel, nr, nc),
            out_shape=jax.ShapeDtypeStruct((1, 1, keep_r, keep_c, width, width), kind),
            in_specs=[large, small, small, small, large, small, small, small, small],
            out_specs=large,
            scratch_shapes=[
                pltpu.VMEM((nc, slots, width, width), kind),
                pltpu.VMEM((nr * depth, width, width), kind),
                pltpu.VMEM((nc * slots + 1, width, width), jnp.float32),
                pltpu.VMEM((keep_r, keep_c, width, width), kind),
                pltpu.VMEM((nc, 8, 128), jnp.int32),
                pltpu.VMEM((nr, 8, 128), jnp.int32),
                pltpu.SMEM((nc, 8, 128), jnp.int32),
                pltpu.SMEM((nr, 8, 128), jnp.int32),
                dma((nc, slots)),
                dma((nc, slots)),
                dma((slots,)),
                dma((nr,)),
                dma((nr,)),
                dma((nc,)),
                dma((nc,)),
                dma((nr,)),
                dma((nr,)),
                dma((2,)),
                dma((2,)),
                dma((keep_r * keep_c,)),
            ],
            compiler_params=pltpu.CompilerParams(
                collective_id=0, has_side_effects=True, vmem_limit_bytes=vmem
            ),
            cost_estimate=pl.CostEstimate(
                flops=2 * nc * slots * width**3, bytes_accessed=8 * block * nc * slots, transcendentals=0
            ),
        )(
            left_blocks,
            left_rows,
            left_cols,
            left_count,
            right_blocks,
            right_rows,
            right_cols,
            kept_rows,
            kept_cols,
        )

    in_specs = (
        P("row", "col", None, None, None),
        P("row", "col", None),
        P("row", "col", None),
        P("row", "col"),
        P("row", "col", None, None, None),
        P("row", "col", None),
        P("row", "col", None),
        P("row", None),
        P("col", None),
    )
    out_specs = P("row", "col", None, None, None, None)
    return jax.shard_map(body, mesh=mesh, in_specs=in_specs, out_specs=out_specs, check_vma=False)
```

```python
import functools

import jax
import jax.numpy as jnp
from jax import lax
from jax.experimental import pallas as pl
from jax.experimental.pallas import tpu as pltpu
from jax.sharding import PartitionSpec as P

RB = 16


def flip(index, mask):
    bit = 1
    moved = index
    while bit <= mask:
        if mask & bit:
            moved = moved + bit - 2 * bit * ((index // bit) % 2)
        bit *= 2
    return moved


def kernel(
    nr,
    nc,
    left_ref,
    lrows_ref,
    lcols_ref,
    lcount_ref,
    right_ref,
    rrows_ref,
    rcols_ref,
    krows_ref,
    kcols_ref,
    out_ref,
    lrows,
    lcols,
    lcount,
    rrows,
    rcols,
    krows,
    kcols,
    lefts,
    rights,
    sums,
    meta_l,
    meta_r,
    small_l,
    small_r,
    l_send,
    l_recv,
    f_send,
    r_send,
    r_recv,
    ml_send,
    ml_recv,
    mr_send,
    mr_recv,
    tiny_sem,
    own_sem,
    small_sem,
):
    me_r = lax.axis_index("row")
    me_c = lax.axis_index("col")
    slots = left_ref.shape[2]
    depth = right_ref.shape[2]
    halves = nr // nc
    keep_r = krows.shape[1]
    keep_c = kcols.shape[1]

    own_left = pltpu.make_async_copy(left_ref.at[0, 0], lefts.at[me_c], own_sem.at[0])
    own_right = pltpu.make_async_copy(
        right_ref.at[0, 0], rights.at[pl.ds(me_r * depth, depth)], own_sem.at[1]
    )
    smalls = [
        pltpu.make_async_copy(src, dst, tiny_sem.at[n])
        for n, (src, dst) in enumerate(
            (
                (lrows_ref, lrows),
                (lcols_ref, lcols),
                (lcount_ref, lcount),
                (rrows_ref, rrows),
                (rcols_ref, rcols),
                (krows_ref, krows),
                (kcols_ref, kcols),
            )
        )
    ]
    for copy in smalls + [own_left, own_right]:
        copy.start()

    barrier = pltpu.get_barrier_semaphore()
    for p in range(1, nc):
        pl.semaphore_signal(
            barrier, inc=1, device_id={"col": flip(me_c, p)}, device_id_type=pl.DeviceIdType.MESH
        )
    for p in range(1, nr):
        pl.semaphore_signal(
            barrier, inc=1, device_id={"row": flip(me_r, p)}, device_id_type=pl.DeviceIdType.MESH
        )

    for copy in smalls:
        copy.wait()

    lane = lax.broadcasted_iota(jnp.int32, meta_l.shape[1:], 1)
    tile = jnp.zeros(meta_l.shape[1:], jnp.int32)
    for a in range(slots):
        tile = jnp.where(lane == a, lrows[0, 0, a], tile)
        tile = jnp.where(lane == slots + a, lcols[0, 0, a], tile)
    tile = jnp.where(lane == 2 * slots, lcount[0, 0], tile)
    base = 2 * slots + 1
    for b in range(depth):
        tile = jnp.where(lane == base + b, rrows[0, 0, b], tile)
        tile = jnp.where(lane == base + depth + b, rcols[0, 0, b], tile)
    meta_l[me_c] = tile
    meta_r[me_r] = tile
    sums[0] = jnp.zeros(sums.shape[1:], sums.dtype)

    pl.semaphore_wait(barrier, nc - 1 + nr - 1)

    def along(axis, peer, src, dst, send, recv):
        return pltpu.make_async_remote_copy(
            src_ref=src,
            dst_ref=dst,
            send_sem=send,
            recv_sem=recv,
            device_id={axis: peer},
            device_id_type=pl.DeviceIdType.MESH,
        )

    sent = []

    relayed = nc % 4 == 0
    half = slots // 2
    first = list(range(half))
    second = list(range(half, slots))
    relay_of = {1: first, 2: second}

    def send_left(p, a):
        copy = along(
            "col",
            flip(me_c, p),
            left_ref.at[0, 0, a],
            lefts.at[me_c, a],
            l_send.at[p, a],
            l_recv.at[p, a],
        )
        copy.start()
        sent.append(copy)

    if relayed:
        for a, b in zip(first + second, second + first) if len(first) == len(second) else []:
            send_left(1, a)
            send_left(2, b)
        if len(first) != len(second):
            for a in first + second:
                send_left(1, a)
            for a in second + first:
                send_left(2, a)
        direct = [p for p in range(4, nc)]
    else:
        direct = [p for p in range(1, nc)]

    def rows_of(q):
        return rights.at[pl.ds(q * depth, depth)]

    for p in [p for p in range(2, nr, 2)] + [1]:
        copy = along(
            "row",
            flip(me_r, p),
            right_ref.at[0, 0],
            rows_of(me_r),
            r_send.at[p],
            r_recv.at[p],
        )
        copy.start()
        sent.append(copy)
    for p in range(1, nr):
        copy = along(
            "row", flip(me_r, p), meta_r.at[me_r], meta_r.at[me_r], mr_send.at[p], mr_recv.at[p]
        )
        copy.start()
        sent.append(copy)
    for p in range(1, nc):
        copy = along(
            "col", flip(me_c, p), meta_l.at[me_c], meta_l.at[me_c], ml_send.at[p], ml_recv.at[p]
        )
        copy.start()
        sent.append(copy)
    for p in direct:
        for a in range(slots):
            send_left(p, a)

    def wait_left(p, a):
        k = flip(me_c, p)
        along(
            "col", k, lefts.at[k, a], lefts.at[k, a], l_send.at[p, a], l_recv.at[p, a]
        ).wait_recv()

    def wait_right(p):
        q = flip(me_r, p)
        along("row", q, rows_of(q), rows_of(q), r_send.at[p], r_recv.at[p]).wait_recv()

    waited = set()

    def pass_left(p, a):
        wait_left(p, a)
        waited.add((p, a))
        k = flip(me_c, p)
        copy = along(
            "col",
            flip(me_c, 3 - p),
            lefts.at[k, a],
            lefts.at[k, a],
            f_send.at[a],
            l_recv.at[3, a],
        )
        copy.start()
        sent.append(copy)

    def pass_right(p):
        wait_right(p)
        q = flip(me_r, p)
        copy = along("row", flip(me_r, 1), rows_of(q), rows_of(q), r_send.at[p + 1], r_recv.at[p + 1])
        copy.start()
        sent.append(copy)

    left_steps = []
    if relayed:
        for n in range(max(len(first), len(second))):
            for p in (1, 2):
                if n < len(relay_of[p]):
                    left_steps.append(functools.partial(pass_left, p, relay_of[p][n]))
    right_steps = [functools.partial(pass_right, p) for p in range(2, nr, 2)]
    while left_steps or right_steps:
        for step in left_steps[:2] + right_steps[:1]:
            step()
        left_steps, right_steps = left_steps[2:], right_steps[1:]

    for p in range(1, nr):
        q = flip(me_r, p)
        along("row", q, meta_r.at[q], meta_r.at[q], mr_send.at[p], mr_recv.at[p]).wait_recv()
    for p in range(1, nc):
        k = flip(me_c, p)
        along("col", k, meta_l.at[k], meta_l.at[k], ml_send.at[p], ml_recv.at[p]).wait_recv()
    to_small = [
        pltpu.make_async_copy(meta_l, small_l, small_sem.at[0]),
        pltpu.make_async_copy(meta_r, small_r, small_sem.at[1]),
    ]
    for copy in to_small:
        copy.start()
    for copy in to_small:
        copy.wait()

    order = [(0, a) for a in range(slots)]
    if relayed:
        order += [(1, a) for a in first] + [(2, a) for a in second]
        order += [(1, a) for a in second] + [(2, a) for a in first]
        for a, b in zip(first, second):
            order += [(3, a), (3, b)]
        order += [(3, a) for a in first[len(second) :] + second[len(first) :]]
    order += [(p, a) for p in direct for a in range(slots)]

    last = {(i, j): jnp.int32(0) for i in range(keep_r) for j in range(keep_c)}
    plan = []
    for t, (p, a) in enumerate(order):
        k = flip(me_c, p)
        row = small_l[k, 0, a]
        contract = small_l[k, 0, slots + a]
        live = a < small_l[k, 0, 2 * slots]
        source = jnp.int32(0)
        column = jnp.int32(-1)
        for u in range(halves):
            q = halves * k + u
            for b in range(depth):
                match = contract == u * RB + small_r[q, 0, base + b]
                source = jnp.where(match, q * depth + b, source)
                column = jnp.where(match, small_r[q, 0, base + depth + b], column)
        before = jnp.int32(0)
        for i in range(keep_r):
            row_on = live & (row == krows[0, i])
            for j in range(keep_c):
                on = row_on & (column == kcols[0, j])
                before = jnp.where(on, last[i, j], before)
                last[i, j] = jnp.where(on, t + 1, last[i, j])
        plan.append((k, source, before))

    own_right.wait()
    for p in [1] + [p for p in range(3, nr, 2)]:
        wait_right(p)
    own_left.wait()
    for t, (p, a) in enumerate(order):
        if p > 0 and (p, a) not in waited:
            wait_left(p, a)
        k, source, before = plan[t]
        sums[t + 1] = sums[before] + jnp.dot(
            lefts[k, a], rights[source], preferred_element_type=jnp.float32
        )

    for i in range(keep_r):
        for j in range(keep_c):
            out_ref[0, 0, i, j] = sums[last[i, j]].astype(out_ref.dtype)
    for copy in sent:
        copy.wait_send()


def solution(mesh):
    nr, nc = mesh.shape["row"], mesh.shape["col"]

    def body(
        left_blocks,
        left_rows,
        left_cols,
        left_count,
        right_blocks,
        right_rows,
        right_cols,
        kept_rows,
        kept_cols,
    ):
        slots, width = left_blocks.shape[2], left_blocks.shape[3]
        depth = right_blocks.shape[2]
        keep_r, keep_c = kept_rows.shape[1], kept_cols.shape[1]
        kind = left_blocks.dtype
        block = width * width
        vmem = (
            2 * block * (nc * slots + nr * depth + keep_r * keep_c)
            + 4 * block * (nc * slots + 1)
            + 4 * 1024 * (nr + nc)
            + (4 << 20)
        )
        smalls = (left_rows, left_cols, left_count, right_rows, right_cols, kept_rows, kept_cols)
        large = pl.BlockSpec(memory_space=pltpu.HBM)
        dma = pltpu.SemaphoreType.DMA
        return pl.pallas_call(
            functools.partial(kernel, nr, nc),
            out_shape=jax.ShapeDtypeStruct((1, 1, keep_r, keep_c, width, width), kind),
            in_specs=[large] * 9,
            out_specs=pl.BlockSpec(memory_space=pltpu.VMEM),
            scratch_shapes=[pltpu.SMEM(array.shape, jnp.int32) for array in smalls]
            + [
                pltpu.VMEM((nc, slots, width, width), kind),
                pltpu.VMEM((nr * depth, width, width), kind),
                pltpu.VMEM((nc * slots + 1, width, width), jnp.float32),
                pltpu.VMEM((nc, 8, 128), jnp.int32),
                pltpu.VMEM((nr, 8, 128), jnp.int32),
                pltpu.SMEM((nc, 8, 128), jnp.int32),
                pltpu.SMEM((nr, 8, 128), jnp.int32),
                dma((nc, slots)),
                dma((nc, slots)),
                dma((slots,)),
                dma((nr,)),
                dma((nr,)),
                dma((nc,)),
                dma((nc,)),
                dma((nr,)),
                dma((nr,)),
                dma((len(smalls),)),
                dma((2,)),
                dma((2,)),
            ],
            compiler_params=pltpu.CompilerParams(
                collective_id=0, has_side_effects=True, vmem_limit_bytes=vmem
            ),
            cost_estimate=pl.CostEstimate(
                flops=2 * nc * slots * width**3, bytes_accessed=8 * block * nc * slots, transcendentals=0
            ),
        )(
            left_blocks,
            left_rows,
            left_cols,
            left_count,
            right_blocks,
            right_rows,
            right_cols,
            kept_rows,
            kept_cols,
        )

    in_specs = (
        P("row", "col", None, None, None),
        P("row", "col", None),
        P("row", "col", None),
        P("row", "col"),
        P("row", "col", None, None, None),
        P("row", "col", None),
        P("row", "col", None),
        P("row", None),
        P("col", None),
    )
    out_specs = P("row", "col", None, None, None, None)
    return jax.shard_map(body, mesh=mesh, in_specs=in_specs, out_specs=out_specs, check_vma=False)
```

```python
import functools

import jax
import jax.numpy as jnp
from jax import lax
from jax.experimental import pallas as pl
from jax.experimental.pallas import tpu as pltpu
from jax.sharding import PartitionSpec as P

RB = 16


def flip(index, mask):
    bit = 1
    moved = index
    while bit <= mask:
        if mask & bit:
            moved = moved + bit - 2 * bit * ((index // bit) % 2)
        bit *= 2
    return moved


def kernel(
    nr,
    nc,
    left_ref,
    lrows_ref,
    lcols_ref,
    lcount_ref,
    right_ref,
    rrows_ref,
    rcols_ref,
    krows_ref,
    kcols_ref,
    out_ref,
    lrows,
    lcols,
    lcount,
    rrows,
    rcols,
    krows,
    kcols,
    lefts,
    rights,
    sums,
    meta_l,
    meta_r,
    small_l,
    small_r,
    l_send,
    l_recv,
    f_send,
    r_send,
    r_recv,
    ml_send,
    ml_recv,
    mr_send,
    mr_recv,
    tiny_sem,
    own_sem,
    small_sem,
):
    me_r = lax.axis_index("row")
    me_c = lax.axis_index("col")
    slots = left_ref.shape[2]
    depth = right_ref.shape[2]
    halves = nr // nc
    keep_r = krows.shape[1]
    keep_c = kcols.shape[1]

    own_left = pltpu.make_async_copy(left_ref.at[0, 0], lefts.at[me_c], own_sem.at[0])
    own_right = pltpu.make_async_copy(
        right_ref.at[0, 0], rights.at[pl.ds(me_r * depth, depth)], own_sem.at[1]
    )
    smalls = [
        pltpu.make_async_copy(src, dst, tiny_sem.at[n])
        for n, (src, dst) in enumerate(
            (
                (lrows_ref, lrows),
                (lcols_ref, lcols),
                (lcount_ref, lcount),
                (rrows_ref, rrows),
                (rcols_ref, rcols),
                (krows_ref, krows),
                (kcols_ref, kcols),
            )
        )
    ]
    for copy in smalls + [own_left, own_right]:
        copy.start()

    barrier = pltpu.get_barrier_semaphore()
    for p in range(1, nc):
        pl.semaphore_signal(
            barrier, inc=1, device_id={"col": flip(me_c, p)}, device_id_type=pl.DeviceIdType.MESH
        )
    for p in range(1, nr):
        pl.semaphore_signal(
            barrier, inc=1, device_id={"row": flip(me_r, p)}, device_id_type=pl.DeviceIdType.MESH
        )

    for copy in smalls:
        copy.wait()

    lane = lax.broadcasted_iota(jnp.int32, meta_l.shape[1:], 1)
    tile = jnp.zeros(meta_l.shape[1:], jnp.int32)
    for a in range(slots):
        tile = jnp.where(lane == a, lrows[0, 0, a], tile)
        tile = jnp.where(lane == slots + a, lcols[0, 0, a], tile)
    tile = jnp.where(lane == 2 * slots, lcount[0, 0], tile)
    base = 2 * slots + 1
    for b in range(depth):
        tile = jnp.where(lane == base + b, rrows[0, 0, b], tile)
        tile = jnp.where(lane == base + depth + b, rcols[0, 0, b], tile)
    meta_l[me_c] = tile
    meta_r[me_r] = tile
    sums[0] = jnp.zeros(sums.shape[1:], sums.dtype)

    pl.semaphore_wait(barrier, nc - 1 + nr - 1)

    def along(axis, peer, src, dst, send, recv):
        return pltpu.make_async_remote_copy(
            src_ref=src,
            dst_ref=dst,
            send_sem=send,
            recv_sem=recv,
            device_id={axis: peer},
            device_id_type=pl.DeviceIdType.MESH,
        )

    sent = []

    for p in range(1, nr):
        copy = along(
            "row", flip(me_r, p), meta_r.at[me_r], meta_r.at[me_r], mr_send.at[p], mr_recv.at[p]
        )
        copy.start()
        sent.append(copy)
    for p in range(1, nc):
        copy = along(
            "col", flip(me_c, p), meta_l.at[me_c], meta_l.at[me_c], ml_send.at[p], ml_recv.at[p]
        )
        copy.start()
        sent.append(copy)

    relayed = nc % 4 == 0
    half = slots // 2
    first = list(range(half))
    second = list(range(half, slots))
    relay_of = {1: first, 2: second}

    def send_left(p, a):
        copy = along(
            "col",
            flip(me_c, p),
            left_ref.at[0, 0, a],
            lefts.at[me_c, a],
            l_send.at[p, a],
            l_recv.at[p, a],
        )
        copy.start()
        sent.append(copy)

    if relayed:
        for a, b in zip(first + second, second + first) if len(first) == len(second) else []:
            send_left(1, a)
            send_left(2, b)
        if len(first) != len(second):
            for a in first + second:
                send_left(1, a)
            for a in second + first:
                send_left(2, a)
        direct = [p for p in range(4, nc)]
    else:
        direct = [p for p in range(1, nc)]

    def rows_of(q):
        return rights.at[pl.ds(q * depth, depth)]

    for p in [p for p in range(2, nr, 2)] + [1]:
        copy = along(
            "row",
            flip(me_r, p),
            right_ref.at[0, 0],
            rows_of(me_r),
            r_send.at[p],
            r_recv.at[p],
        )
        copy.start()
        sent.append(copy)
    for p in direct:
        for a in range(slots):
            send_left(p, a)

    def wait_left(p, a):
        k = flip(me_c, p)
        along(
            "col", k, lefts.at[k, a], lefts.at[k, a], l_send.at[p, a], l_recv.at[p, a]
        ).wait_recv()

    def wait_right(p):
        q = flip(me_r, p)
        along("row", q, rows_of(q), rows_of(q), r_send.at[p], r_recv.at[p]).wait_recv()

    waited = set()

    def pass_left(p, a):
        wait_left(p, a)
        waited.add((p, a))
        k = flip(me_c, p)
        copy = along(
            "col",
            flip(me_c, 3 - p),
            lefts.at[k, a],
            lefts.at[k, a],
            f_send.at[a],
            l_recv.at[3, a],
        )
        copy.start()
        sent.append(copy)

    def pass_right(p):
        wait_right(p)
        q = flip(me_r, p)
        copy = along("row", flip(me_r, 1), rows_of(q), rows_of(q), r_send.at[p + 1], r_recv.at[p + 1])
        copy.start()
        sent.append(copy)

    left_steps = []
    if relayed:
        for n in range(max(len(first), len(second))):
            for p in (1, 2):
                if n < len(relay_of[p]):
                    left_steps.append(functools.partial(pass_left, p, relay_of[p][n]))
    right_steps = [functools.partial(pass_right, p) for p in range(2, nr, 2)]
    while left_steps or right_steps:
        for step in left_steps[:2] + right_steps[:1]:
            step()
        left_steps, right_steps = left_steps[2:], right_steps[1:]

    for p in range(1, nr):
        q = flip(me_r, p)
        along("row", q, meta_r.at[q], meta_r.at[q], mr_send.at[p], mr_recv.at[p]).wait_recv()
    for p in range(1, nc):
        k = flip(me_c, p)
        along("col", k, meta_l.at[k], meta_l.at[k], ml_send.at[p], ml_recv.at[p]).wait_recv()
    to_small = [
        pltpu.make_async_copy(meta_l, small_l, small_sem.at[0]),
        pltpu.make_async_copy(meta_r, small_r, small_sem.at[1]),
    ]
    for copy in to_small:
        copy.start()
    for copy in to_small:
        copy.wait()

    order = [(0, a) for a in range(slots)]
    if relayed:
        order += [(1, a) for a in first] + [(2, a) for a in second]
        order += [(1, a) for a in second] + [(2, a) for a in first]
        for a, b in zip(first, second):
            order += [(3, a), (3, b)]
        order += [(3, a) for a in first[len(second) :] + second[len(first) :]]
    order += [(p, a) for p in direct for a in range(slots)]

    last = {(i, j): jnp.int32(0) for i in range(keep_r) for j in range(keep_c)}
    plan = []
    for t, (p, a) in enumerate(order):
        k = flip(me_c, p)
        row = small_l[k, 0, a]
        contract = small_l[k, 0, slots + a]
        live = a < small_l[k, 0, 2 * slots]
        source = jnp.int32(0)
        column = jnp.int32(-1)
        for u in range(halves):
            q = halves * k + u
            for b in range(depth):
                match = contract == u * RB + small_r[q, 0, base + b]
                source = jnp.where(match, q * depth + b, source)
                column = jnp.where(match, small_r[q, 0, base + depth + b], column)
        before = jnp.int32(0)
        for i in range(keep_r):
            row_on = live & (row == krows[0, i])
            for j in range(keep_c):
                on = row_on & (column == kcols[0, j])
                before = jnp.where(on, last[i, j], before)
                last[i, j] = jnp.where(on, t + 1, last[i, j])
        plan.append((k, source, before))

    own_right.wait()
    for p in [1] + [p for p in range(3, nr, 2)]:
        wait_right(p)
    own_left.wait()
    for t, (p, a) in enumerate(order):
        if p > 0 and (p, a) not in waited:
            wait_left(p, a)
        k, source, before = plan[t]
        sums[t + 1] = sums[before] + jnp.dot(
            lefts[k, a], rights[source], preferred_element_type=jnp.float32
        )

    for i in range(keep_r):
        for j in range(keep_c):
            out_ref[0, 0, i, j] = sums[last[i, j]].astype(out_ref.dtype)
    for copy in sent:
        copy.wait_send()


def solution(mesh):
    nr, nc = mesh.shape["row"], mesh.shape["col"]

    def body(
        left_blocks,
        left_rows,
        left_cols,
        left_count,
        right_blocks,
        right_rows,
        right_cols,
        kept_rows,
        kept_cols,
    ):
        slots, width = left_blocks.shape[2], left_blocks.shape[3]
        depth = right_blocks.shape[2]
        keep_r, keep_c = kept_rows.shape[1], kept_cols.shape[1]
        kind = left_blocks.dtype
        block = width * width
        vmem = (
            2 * block * (nc * slots + nr * depth + keep_r * keep_c)
            + 4 * block * (nc * slots + 1)
            + 4 * 1024 * (nr + nc)
            + (4 << 20)
        )
        smalls = (left_rows, left_cols, left_count, right_rows, right_cols, kept_rows, kept_cols)
        large = pl.BlockSpec(memory_space=pltpu.HBM)
        dma = pltpu.SemaphoreType.DMA
        return pl.pallas_call(
            functools.partial(kernel, nr, nc),
            out_shape=jax.ShapeDtypeStruct((1, 1, keep_r, keep_c, width, width), kind),
            in_specs=[large] * 9,
            out_specs=pl.BlockSpec(memory_space=pltpu.VMEM),
            scratch_shapes=[pltpu.SMEM(array.shape, jnp.int32) for array in smalls]
            + [
                pltpu.VMEM((nc, slots, width, width), kind),
                pltpu.VMEM((nr * depth, width, width), kind),
                pltpu.VMEM((nc * slots + 1, width, width), jnp.float32),
                pltpu.VMEM((nc, 8, 128), jnp.int32),
                pltpu.VMEM((nr, 8, 128), jnp.int32),
                pltpu.SMEM((nc, 8, 128), jnp.int32),
                pltpu.SMEM((nr, 8, 128), jnp.int32),
                dma((nc, slots)),
                dma((nc, slots)),
                dma((slots,)),
                dma((nr,)),
                dma((nr,)),
                dma((nc,)),
                dma((nc,)),
                dma((nr,)),
                dma((nr,)),
                dma((len(smalls),)),
                dma((2,)),
                dma((2,)),
            ],
            compiler_params=pltpu.CompilerParams(
                collective_id=0, has_side_effects=True, vmem_limit_bytes=vmem
            ),
            cost_estimate=pl.CostEstimate(
                flops=2 * nc * slots * width**3, bytes_accessed=8 * block * nc * slots, transcendentals=0
            ),
        )(
            left_blocks,
            left_rows,
            left_cols,
            left_count,
            right_blocks,
            right_rows,
            right_cols,
            kept_rows,
            kept_cols,
        )

    in_specs = (
        P("row", "col", None, None, None),
        P("row", "col", None),
        P("row", "col", None),
        P("row", "col"),
        P("row", "col", None, None, None),
        P("row", "col", None),
        P("row", "col", None),
        P("row", None),
        P("col", None),
    )
    out_specs = P("row", "col", None, None, None, None)
    return jax.shard_map(body, mesh=mesh, in_specs=in_specs, out_specs=out_specs, check_vma=False)
```

```python
import functools

import jax
import jax.numpy as jnp
from jax import lax
from jax.experimental import pallas as pl
from jax.experimental.pallas import tpu as pltpu
from jax.sharding import PartitionSpec as P

RB = 16


def flip(index, mask):
    bit = 1
    moved = index
    while bit <= mask:
        if mask & bit:
            moved = moved + bit - 2 * bit * ((index // bit) % 2)
        bit *= 2
    return moved


def kernel(
    nr,
    nc,
    left_ref,
    lrows_ref,
    lcols_ref,
    lcount_ref,
    right_ref,
    rrows_ref,
    rcols_ref,
    krows_ref,
    kcols_ref,
    out_ref,
    lrows,
    lcols,
    lcount,
    rrows,
    rcols,
    krows,
    kcols,
    lefts,
    rights,
    sums,
    meta_l,
    meta_r,
    small_l,
    small_r,
    l_send,
    l_recv,
    f_send,
    r_send,
    r_recv,
    ml_send,
    ml_recv,
    mr_send,
    mr_recv,
    tiny_sem,
    own_sem,
    small_sem,
):
    me_r = lax.axis_index("row")
    me_c = lax.axis_index("col")
    slots = left_ref.shape[2]
    depth = right_ref.shape[2]
    halves = nr // nc
    keep_r = krows.shape[1]
    keep_c = kcols.shape[1]

    barrier = pltpu.get_barrier_semaphore()
    for p in range(1, nc):
        pl.semaphore_signal(
            barrier, inc=1, device_id={"col": flip(me_c, p)}, device_id_type=pl.DeviceIdType.MESH
        )
    for p in range(1, nr):
        pl.semaphore_signal(
            barrier, inc=1, device_id={"row": flip(me_r, p)}, device_id_type=pl.DeviceIdType.MESH
        )

    own_left = pltpu.make_async_copy(left_ref.at[0, 0], lefts.at[me_c], own_sem.at[0])
    own_right = pltpu.make_async_copy(
        right_ref.at[0, 0], rights.at[pl.ds(me_r * depth, depth)], own_sem.at[1]
    )
    smalls = [
        pltpu.make_async_copy(src, dst, tiny_sem.at[n])
        for n, (src, dst) in enumerate(
            (
                (lrows_ref, lrows),
                (lcols_ref, lcols),
                (lcount_ref, lcount),
                (rrows_ref, rrows),
                (rcols_ref, rcols),
                (krows_ref, krows),
                (kcols_ref, kcols),
            )
        )
    ]
    for copy in smalls:
        copy.start()
    for copy in smalls:
        copy.wait()

    lane = lax.broadcasted_iota(jnp.int32, meta_l.shape[1:], 1)
    tile = jnp.zeros(meta_l.shape[1:], jnp.int32)
    for a in range(slots):
        tile = jnp.where(lane == a, lrows[0, 0, a], tile)
        tile = jnp.where(lane == slots + a, lcols[0, 0, a], tile)
    tile = jnp.where(lane == 2 * slots, lcount[0, 0], tile)
    base = 2 * slots + 1
    for b in range(depth):
        tile = jnp.where(lane == base + b, rrows[0, 0, b], tile)
        tile = jnp.where(lane == base + depth + b, rcols[0, 0, b], tile)
    meta_l[me_c] = tile
    meta_r[me_r] = tile
    sums[0] = jnp.zeros(sums.shape[1:], sums.dtype)

    pl.semaphore_wait(barrier, nc - 1 + nr - 1)

    def along(axis, peer, src, dst, send, recv):
        return pltpu.make_async_remote_copy(
            src_ref=src,
            dst_ref=dst,
            send_sem=send,
            recv_sem=recv,
            device_id={axis: peer},
            device_id_type=pl.DeviceIdType.MESH,
        )

    sent = []

    for p in range(1, nr):
        copy = along(
            "row", flip(me_r, p), meta_r.at[me_r], meta_r.at[me_r], mr_send.at[p], mr_recv.at[p]
        )
        copy.start()
        sent.append(copy)
    for p in range(1, nc):
        copy = along(
            "col", flip(me_c, p), meta_l.at[me_c], meta_l.at[me_c], ml_send.at[p], ml_recv.at[p]
        )
        copy.start()
        sent.append(copy)

    relayed = nc % 4 == 0
    half = slots // 2
    first = list(range(half))
    second = list(range(half, slots))
    relay_of = {1: first, 2: second}

    def send_left(p, a):
        copy = along(
            "col",
            flip(me_c, p),
            left_ref.at[0, 0, a],
            lefts.at[me_c, a],
            l_send.at[p, a],
            l_recv.at[p, a],
        )
        copy.start()
        sent.append(copy)

    if relayed:
        for a, b in zip(first + second, second + first) if len(first) == len(second) else []:
            send_left(1, a)
            send_left(2, b)
        if len(first) != len(second):
            for a in first + second:
                send_left(1, a)
            for a in second + first:
                send_left(2, a)
        direct = [p for p in range(4, nc)]
    else:
        direct = [p for p in range(1, nc)]

    def rows_of(q):
        return rights.at[pl.ds(q * depth, depth)]

    for p in [p for p in range(2, nr, 2)] + [1]:
        copy = along(
            "row",
            flip(me_r, p),
            right_ref.at[0, 0],
            rows_of(me_r),
            r_send.at[p],
            r_recv.at[p],
        )
        copy.start()
        sent.append(copy)
    for p in direct:
        for a in range(slots):
            send_left(p, a)

    own_left.start()
    own_right.start()

    def wait_left(p, a):
        k = flip(me_c, p)
        along(
            "col", k, lefts.at[k, a], lefts.at[k, a], l_send.at[p, a], l_recv.at[p, a]
        ).wait_recv()

    def wait_right(p):
        q = flip(me_r, p)
        along("row", q, rows_of(q), rows_of(q), r_send.at[p], r_recv.at[p]).wait_recv()

    waited = set()

    def pass_left(p, a):
        wait_left(p, a)
        waited.add((p, a))
        k = flip(me_c, p)
        copy = along(
            "col",
            flip(me_c, 3 - p),
            lefts.at[k, a],
            lefts.at[k, a],
            f_send.at[a],
            l_recv.at[3, a],
        )
        copy.start()
        sent.append(copy)

    def pass_right(p):
        wait_right(p)
        q = flip(me_r, p)
        copy = along("row", flip(me_r, 1), rows_of(q), rows_of(q), r_send.at[p + 1], r_recv.at[p + 1])
        copy.start()
        sent.append(copy)

    left_steps = []
    if relayed:
        for n in range(max(len(first), len(second))):
            for p in (1, 2):
                if n < len(relay_of[p]):
                    left_steps.append(functools.partial(pass_left, p, relay_of[p][n]))
    right_steps = [functools.partial(pass_right, p) for p in range(2, nr, 2)]
    while left_steps or right_steps:
        for step in left_steps[:2] + right_steps[:1]:
            step()
        left_steps, right_steps = left_steps[2:], right_steps[1:]

    for p in range(1, nr):
        q = flip(me_r, p)
        along("row", q, meta_r.at[q], meta_r.at[q], mr_send.at[p], mr_recv.at[p]).wait_recv()
    for p in range(1, nc):
        k = flip(me_c, p)
        along("col", k, meta_l.at[k], meta_l.at[k], ml_send.at[p], ml_recv.at[p]).wait_recv()
    to_small = [
        pltpu.make_async_copy(meta_l, small_l, small_sem.at[0]),
        pltpu.make_async_copy(meta_r, small_r, small_sem.at[1]),
    ]
    for copy in to_small:
        copy.start()
    for copy in to_small:
        copy.wait()

    order = [(0, a) for a in range(slots)]
    if relayed:
        order += [(1, a) for a in first] + [(2, a) for a in second]
        order += [(1, a) for a in second] + [(2, a) for a in first]
        for a, b in zip(first, second):
            order += [(3, a), (3, b)]
        order += [(3, a) for a in first[len(second) :] + second[len(first) :]]
    order += [(p, a) for p in direct for a in range(slots)]

    last = {(i, j): jnp.int32(0) for i in range(keep_r) for j in range(keep_c)}
    plan = []
    for t, (p, a) in enumerate(order):
        k = flip(me_c, p)
        row = small_l[k, 0, a]
        contract = small_l[k, 0, slots + a]
        live = a < small_l[k, 0, 2 * slots]
        source = jnp.int32(0)
        column = jnp.int32(-1)
        for u in range(halves):
            q = halves * k + u
            for b in range(depth):
                match = contract == u * RB + small_r[q, 0, base + b]
                source = jnp.where(match, q * depth + b, source)
                column = jnp.where(match, small_r[q, 0, base + depth + b], column)
        before = jnp.int32(0)
        for i in range(keep_r):
            row_on = live & (row == krows[0, i])
            for j in range(keep_c):
                on = row_on & (column == kcols[0, j])
                before = jnp.where(on, last[i, j], before)
                last[i, j] = jnp.where(on, t + 1, last[i, j])
        plan.append((k, source, before))

    own_right.wait()
    for p in [1] + [p for p in range(3, nr, 2)]:
        wait_right(p)
    own_left.wait()
    for t, (p, a) in enumerate(order):
        if p > 0 and (p, a) not in waited:
            wait_left(p, a)
        k, source, before = plan[t]
        sums[t + 1] = sums[before] + jnp.dot(
            lefts[k, a], rights[source], preferred_element_type=jnp.float32
        )

    for i in range(keep_r):
        for j in range(keep_c):
            out_ref[0, 0, i, j] = sums[last[i, j]].astype(out_ref.dtype)
    for copy in sent:
        copy.wait_send()


def solution(mesh):
    nr, nc = mesh.shape["row"], mesh.shape["col"]

    def body(
        left_blocks,
        left_rows,
        left_cols,
        left_count,
        right_blocks,
        right_rows,
        right_cols,
        kept_rows,
        kept_cols,
    ):
        slots, width = left_blocks.shape[2], left_blocks.shape[3]
        depth = right_blocks.shape[2]
        keep_r, keep_c = kept_rows.shape[1], kept_cols.shape[1]
        kind = left_blocks.dtype
        block = width * width
        vmem = (
            2 * block * (nc * slots + nr * depth + keep_r * keep_c)
            + 4 * block * (nc * slots + 1)
            + 4 * 1024 * (nr + nc)
            + (4 << 20)
        )
        smalls = (left_rows, left_cols, left_count, right_rows, right_cols, kept_rows, kept_cols)
        large = pl.BlockSpec(memory_space=pltpu.HBM)
        dma = pltpu.SemaphoreType.DMA
        return pl.pallas_call(
            functools.partial(kernel, nr, nc),
            out_shape=jax.ShapeDtypeStruct((1, 1, keep_r, keep_c, width, width), kind),
            in_specs=[large] * 9,
            out_specs=pl.BlockSpec(memory_space=pltpu.VMEM),
            scratch_shapes=[pltpu.SMEM(array.shape, jnp.int32) for array in smalls]
            + [
                pltpu.VMEM((nc, slots, width, width), kind),
                pltpu.VMEM((nr * depth, width, width), kind),
                pltpu.VMEM((nc * slots + 1, width, width), jnp.float32),
                pltpu.VMEM((nc, 8, 128), jnp.int32),
                pltpu.VMEM((nr, 8, 128), jnp.int32),
                pltpu.SMEM((nc, 8, 128), jnp.int32),
                pltpu.SMEM((nr, 8, 128), jnp.int32),
                dma((nc, slots)),
                dma((nc, slots)),
                dma((slots,)),
                dma((nr,)),
                dma((nr,)),
                dma((nc,)),
                dma((nc,)),
                dma((nr,)),
                dma((nr,)),
                dma((len(smalls),)),
                dma((2,)),
                dma((2,)),
            ],
            compiler_params=pltpu.CompilerParams(
                collective_id=0, has_side_effects=True, vmem_limit_bytes=vmem
            ),
            cost_estimate=pl.CostEstimate(
                flops=2 * nc * slots * width**3, bytes_accessed=8 * block * nc * slots, transcendentals=0
            ),
        )(
            left_blocks,
            left_rows,
            left_cols,
            left_count,
            right_blocks,
            right_rows,
            right_cols,
            kept_rows,
            kept_cols,
        )

    in_specs = (
        P("row", "col", None, None, None),
        P("row", "col", None),
        P("row", "col", None),
        P("row", "col"),
        P("row", "col", None, None, None),
        P("row", "col", None),
        P("row", "col", None),
        P("row", None),
        P("col", None),
    )
    out_specs = P("row", "col", None, None, None, None)
    return jax.shard_map(body, mesh=mesh, in_specs=in_specs, out_specs=out_specs, check_vma=False)
```
